32 devices in a mesh: freq: 4 (over z), tile: 8 (over y, x, core).
Axes of the slice: x: 2, y: 2, z: 4, core: 2. Of those that a mesh axis runs over, the one named last changes fastest.
Arguments:
- sources: bfloat16 [4, 2, 4096, 256], P('freq', None, 'tile'), may hold values from -6 to 6
- u_factor: bfloat16 [4, 2, 4096, 1024], P('freq', None, 'tile'), may hold values from -0.125 to 0.125
- v_factor: bfloat16 [4, 2, 4096, 1024], P('freq', None, 'tile'), may hold values from -0.25 to 0.25
- tile_ranks: int32 [16, 16], replicated, may hold values from 32 to 64
- window_start: int32 [4096], P('tile'), may hold values from 0 to 3
- window_end: int32 [4096], P('tile'), may hold values from 5 to 8
Outputs:
- adjoint: bfloat16 [4, 2, 4096, 256], P('freq', None, 'tile')
The draws below stay inside these ranges and needn't reach their ends.
Inputs may be any that keep to these rules, and one draw needn't show every extreme that they name: `tile_ranks`: the number of leading coefficients of tile (i, j) in use.
All inputs are finite; a program needn't handle non-finite values.
Results may differ from the reference program's by a relative error of at most 0.01.
Values may be sent and summed in bfloat16 or wider, within the bound.
A program may use at most 128 MiB of HBM per device.

```python
import math
import jax
import jax.numpy as jnp
from jax import lax

B = 256
R = 64
S = 256
TILES = 16
FREQS = 4
TIMES = 8
N = 4096


def with_ends(drawn, rng, low, high):
    dims = drawn.shape
    index_at = [jax.random.randint(jax.random.fold_in(rng, axis), (), 0, dims[axis]) for axis in range(len(dims))]
    drawn = drawn.at[tuple(index_at)].set(low)
    longest = dims.index(max(dims))
    index_at[longest] = (index_at[longest] + 1) % dims[longest]
    return drawn.at[tuple(index_at)].set(high)


def block_levels(rng, shape, split, least, largest):
    level, own = 1.0, jax.random.fold_in(rng, 6)
    for axis_at, blocks in split:
        steps = jnp.exp(jax.random.uniform(jax.random.fold_in(own, axis_at), (blocks,), jnp.float32, least / len(split), largest / len(split)))
        level = level * jnp.repeat(steps, shape[axis_at] // blocks).reshape([-1 if axis == axis_at else 1 for axis in range(len(shape))])
    return level


def bell_draw(key, shape, scale, most, pieces=(), held_as=jnp.bfloat16):
    drawn = scale * jax.random.normal(key, shape, jnp.float32)
    if pieces:
        drawn = drawn * block_levels(key, shape, pieces, -0.22, 0.18)
    return jnp.clip(drawn, -most, most).astype(held_as)


def setup_inputs(seed: int = 0) -> dict:
    streams_of = jax.random.split(jax.random.key(seed), 7)
    return {
        "sources": bell_draw(streams_of[0], (FREQS, 2, N, S), 1.0, 6.0, ((0, 4), (2, 8))),
        "u_factor": bell_draw(streams_of[1], (FREQS, 2, N, TILES * R), (2 * TILES * R) ** -0.5, 0.125, ((0, 4), (2, 8))),
        "v_factor": bell_draw(streams_of[2], (FREQS, 2, N, TILES * R), (2 * B) ** -0.5, 0.25, ((0, 4), (2, 8))),
        "tile_ranks": with_ends(jax.random.randint(streams_of[3], (TILES, TILES), R // 2, R + 1), jax.random.fold_in(streams_of[3], 1), R // 2, R).astype(jnp.int32),
        "window_start": with_ends(jax.random.randint(streams_of[4], (N,), 0, TIMES // 2), jax.random.fold_in(streams_of[4], 1), 0, (TIMES // 2) - 1).astype(jnp.int32),
        "window_end": with_ends(jax.random.randint(streams_of[5], (N,), TIMES // 2 + 1, TIMES + 1), jax.random.fold_in(streams_of[5], 1), TIMES // 2 + 1, TIMES).astype(jnp.int32),
    }


def product(pattern, left_op, right_op):
    return jnp.einsum(pattern, left_op.astype(jnp.float32), right_op.astype(jnp.float32))

def precise(pattern, left_op, right_op):
    return jnp.einsum(pattern, left_op, right_op, precision=lax.Precision.HIGHEST)

def phase_tables(freq_count, time_count):
    moment = jnp.arange(time_count, dtype=jnp.int32)[:, None]
    freq_col = jnp.arange(freq_count, dtype=jnp.int32)[None, :]
    angles = (moment * freq_col % time_count).astype(jnp.float32) * (2.0 * math.pi / time_count)
    scaling = 1.0 / math.sqrt(freq_count)
    return (jnp.cos(angles) * scaling, jnp.sin(angles) * scaling)

def reference(sources, u_factor, v_factor, tile_ranks, window_start, window_end):
    retained = (jnp.arange(R, dtype=jnp.int32)[None, None, :] < tile_ranks[:, :, None]).astype(jnp.float32)

    def forward(triple):
        shot_block, u_block, v_block = triple
        shot_grid = shot_block.astype(jnp.float32).reshape(2, TILES, B, S)
        v_grid = v_block.astype(jnp.float32).reshape(2, TILES, B, TILES, R)
        coef_real = product('jbir,jbs->ijrs', v_grid[0], shot_grid[0]) + product('jbir,jbs->ijrs', v_grid[1], shot_grid[1])
        coef_imag = product('jbir,jbs->ijrs', v_grid[0], shot_grid[1]) - product('jbir,jbs->ijrs', v_grid[1], shot_grid[0])
        coefficients = (jnp.stack([coef_real, coef_imag]) * retained[None, :, :, :, None]).astype(jnp.bfloat16)
        coef_grid = lax.optimization_barrier(coefficients).astype(jnp.float32)
        u_grid = u_block.astype(jnp.float32).reshape(2, TILES, B, TILES, R)
        data_real = product('ibjr,ijrs->ibs', u_grid[0], coef_grid[0]) - product('ibjr,ijrs->ibs', u_grid[1], coef_grid[1])
        data_imag = product('ibjr,ijrs->ibs', u_grid[0], coef_grid[1]) + product('ibjr,ijrs->ibs', u_grid[1], coef_grid[0])
        return jnp.stack([data_real, data_imag]).reshape(2, TILES * B, S).astype(jnp.bfloat16)
    recorded = lax.map(forward, (sources, u_factor, v_factor))
    cos_table, sin_table = phase_tables(FREQS, TIMES)
    freq_data = recorded.astype(jnp.float32)
    time_real = precise('tf,fns->tns', cos_table, freq_data[:, 0]) - precise('tf,fns->tns', sin_table, freq_data[:, 1])
    time_imag = precise('tf,fns->tns', cos_table, freq_data[:, 1]) + precise('tf,fns->tns', sin_table, freq_data[:, 0])
    moments = jnp.arange(TIMES, dtype=jnp.int32)[:, None]
    window = ((moments >= window_start[None, :]) & (moments < window_end[None, :])).astype(jnp.float32)[:, :, None]
    time_real = time_real * window
    time_imag = time_imag * window
    back_real = precise('tf,tns->fns', cos_table, time_real) + precise('tf,tns->fns', sin_table, time_imag)
    back_imag = precise('tf,tns->fns', cos_table, time_imag) - precise('tf,tns->fns', sin_table, time_real)
    windowed = jnp.stack([back_real, back_imag], axis=1).astype(jnp.bfloat16)

    def adjoint_pass(triple):
        w_block, u_block, v_block = triple
        w_grid = w_block.astype(jnp.float32).reshape(2, TILES, B, S)
        u_grid = u_block.astype(jnp.float32).reshape(2, TILES, B, TILES, R)
        adj_real = product('ibjr,ibs->ijrs', u_grid[0], w_grid[0]) + product('ibjr,ibs->ijrs', u_grid[1], w_grid[1])
        adj_imag = product('ibjr,ibs->ijrs', u_grid[0], w_grid[1]) - product('ibjr,ibs->ijrs', u_grid[1], w_grid[0])
        adj_coef = (jnp.stack([adj_real, adj_imag]) * retained[None, :, :, :, None]).astype(jnp.bfloat16)
        adj_grid = lax.optimization_barrier(adj_coef).astype(jnp.float32)
        v_grid = v_block.astype(jnp.float32).reshape(2, TILES, B, TILES, R)
        out_real = product('jbir,ijrs->jbs', v_grid[0], adj_grid[0]) - product('jbir,ijrs->jbs', v_grid[1], adj_grid[1])
        out_imag = product('jbir,ijrs->jbs', v_grid[0], adj_grid[1]) + product('jbir,ijrs->jbs', v_grid[1], adj_grid[0])
        return jnp.stack([out_real, out_imag]).reshape(2, TILES * B, S).astype(jnp.bfloat16)
    return lax.map(adjoint_pass, (windowed, u_factor, v_factor))
```

```python
import functools
import math

import jax
import jax.numpy as jnp
from jax import lax
from jax.experimental import pallas as pl
from jax.experimental.pallas import tpu as pltpu
from jax.sharding import PartitionSpec as P

B = 256
R = 64
CHUNKS = 2
MESH = pl.DeviceIdType.MESH


def dot(a, b):
    return jnp.dot(a, b, preferred_element_type=jnp.float32)


def dot_nt(a, b):
    return lax.dot_general(a, b, (((1,), (1,)), ((), ())), preferred_element_type=jnp.float32)


def kernel(
    n, groups, src_hbm, u_hbm, v_hbm, ranks, start_ref, end_ref, out_ref,
    src, u, v, xt, t_out, t_in, z_out, z_in, kbuf,
    in_sem, t_send, t_recv, z_send, z_recv,
):
    me = lax.axis_index("tile")
    mf = lax.axis_index("freq")
    span = src.shape[1]
    shots = src.shape[2]
    tiles = span // B
    lanes = tiles * R
    chunks = t_out.shape[1]
    width = shots // chunks
    piece = width // groups
    pairs = n // 2
    my_pair = lax.div(me, 2)
    sibling = me + 1 - 2 * lax.rem(me, 2)

    barrier = pltpu.get_barrier_semaphore()
    for r in range(1, n):
        pl.semaphore_signal(barrier, inc=1, device_id=(mf, lax.rem(me + r, n)), device_id_type=MESH)
    for r in range(1, groups):
        pl.semaphore_signal(
            barrier, inc=1, device_id=(lax.rem(mf + r, groups), me), device_id_type=MESH
        )
    loads = [
        pltpu.make_async_copy(a, b, in_sem.at[k])
        for k, (a, b) in enumerate(((src_hbm, src), (v_hbm, v), (u_hbm, u)))
    ]
    for copy in loads:
        copy.start()

    times = 2 * groups
    first, last = start_ref[...], end_ref[...]
    inside = [((first <= t) & (last > t)).astype(jnp.float32) for t in range(times)]
    for d in range(groups):
        real = imag = jnp.zeros_like(inside[0])
        for t in range(times):
            angle = 2.0 * math.pi * ((t * d) % times) / times
            real += inside[t] * (math.cos(angle) / groups)
            imag += inside[t] * (math.sin(angle) / groups)
        kbuf[2 * d] = real
        kbuf[2 * d + 1] = imag

    loads[0].wait()
    for c in range(chunks):
        for j in range(tiles):
            part = [
                src[k, j * B : (j + 1) * B, c * width : (c + 1) * width].astype(jnp.float32).T
                for k in range(2)
            ]
            xt[c, j, 0, :width] = part[0].astype(jnp.bfloat16)
            xt[c, j, 0, width:] = part[1].astype(jnp.bfloat16)
            xt[c, j, 1, :width] = part[1].astype(jnp.bfloat16)
            xt[c, j, 1, width:] = (-part[0]).astype(jnp.bfloat16)
    loads[1].wait()

    lane = lax.broadcasted_iota(jnp.int32, (1, lanes), 1)
    low = lane < R
    within = lax.rem(lane, R)

    def t_copy(phase, c, r):
        pair = lax.rem(my_pair + lax.div(r, 2), pairs)
        target = jnp.where(lax.div(r, 2) == 0, sibling, 2 * pair + lax.rem(r, 2))
        return pltpu.make_async_remote_copy(
            src_ref=t_out.at[phase, c, target],
            dst_ref=t_in.at[phase, c, me],
            send_sem=t_send.at[phase, c, r],
            recv_sem=t_recv.at[phase, c, me],
            device_id=(mf, target),
            device_id_type=MESH,
        )

    def t_arrived(phase, c, source):
        return pltpu.make_async_remote_copy(
            src_ref=t_out.at[phase, c, source],
            dst_ref=t_in.at[phase, c, source],
            send_sem=t_send.at[phase, c, 0],
            recv_sem=t_recv.at[phase, c, source],
            device_id=(mf, source),
            device_id_type=MESH,
        )

    def blocks(phase, c, pair, operands, weights, put):
        columns = pl.ds(pl.multiple_of(pair * 2 * lanes, 2 * lanes), 2 * lanes)
        full = [
            dot(operands(k, 0), weights[0, k * B : (k + 1) * B, columns])
            + dot(operands(k, 1), weights[1, k * B : (k + 1) * B, columns])
            for k in range(tiles)
        ]
        for h in range(2):
            dest = 2 * pair + h
            own, other = (f[:, h * lanes : (h + 1) * lanes] for f in full)
            mixed = (
                jnp.where(low, own, pltpu.roll(other, R, 1)),
                jnp.where(low, pltpu.roll(own, R, 1), other),
            )
            for k in range(tiles):
                theirs = dest * tiles + k
                if phase == 0:
                    rank = [ranks[theirs, me * tiles + m] for m in range(tiles)]
                else:
                    rank = [ranks[me * tiles + m, theirs] for m in range(tiles)]
                keep = within < jnp.where(low, rank[0], rank[1])
                put(dest, k, jnp.where(keep, mixed[k], 0.0).astype(jnp.bfloat16))

    def produce(phase, c, operands, weights, begin, before=None):
        def put(dest, k, value):
            t_out[phase, c, dest, k] = value

        def step(k, carry):
            blocks(phase, c, lax.rem(my_pair + k, pairs), operands, weights, put)
            for h in range(2):
                if before is not None:
                    before(2 * k + h)
                if begin:
                    t_copy(phase, c, 2 * k + h).start()
            return carry

        lax.fori_loop(1, pairs, step, 0)
        blocks(phase, c, my_pair, operands, weights, put)
        t_in[phase, c, me] = t_out[phase, c, me]
        if before is not None:
            before(0)
        if begin:
            t_copy(phase, c, 0).start()

    def each_send(do):
        def step(r, carry):
            do(r)
            return carry

        lax.fori_loop(2, n, step, 0)
        do(0)

    def await_tiles(phase, c):
        def step(r, carry):
            t_arrived(phase, c, lax.rem(me + r, n)).wait_recv()
            return carry

        lax.fori_loop(1, n, step, 0)

    def gathered(phase, c, k):
        whole = jnp.concatenate([t_in[phase, c, s, k] for s in range(n)], axis=1)
        turned = jnp.concatenate([-whole[width:], whole[:width]], axis=0)
        return whole, turned

    def z_copy(phase, c, r):
        target = lax.rem(mf + r, groups)
        return pltpu.make_async_remote_copy(
            src_ref=z_out.at[phase, c, target],
            dst_ref=z_in.at[phase, c, mf],
            send_sem=z_send.at[phase, c, r],
            recv_sem=z_recv.at[phase, c, mf],
            device_id=(target, me),
            device_id_type=MESH,
        )

    def z_arrived(phase, c, source):
        return pltpu.make_async_remote_copy(
            src_ref=z_out.at[phase, c, source],
            dst_ref=z_in.at[phase, c, source],
            send_sem=z_send.at[phase, c, 0],
            recv_sem=z_recv.at[phase, c, source],
            device_id=(source, me),
            device_id_type=MESH,
        )

    def z_start(phase, c):
        for r in range(1, groups):
            z_copy(phase, c, r).start()
        z_in[phase, c, mf] = z_out[phase, c, mf]

    def z_wait(phase, c):
        for r in range(1, groups):
            z_arrived(phase, c, lax.rem(mf + r, groups)).wait_recv()

    def record(c):
        for i in range(tiles):
            whole, turned = gathered(0, c, i)
            rows = slice(i * B, (i + 1) * B)
            result = (dot_nt(whole, u[0, rows, :]) + dot_nt(turned, u[1, rows, :])).astype(
                jnp.bfloat16
            )
            for g in range(groups):
                for k in range(2):
                    at = k * width + g * piece
                    z_out[0, c, g, k, :, rows] = result[at : at + piece]

    def window(c):
        def step(b, carry):
            at = pl.ds(pl.multiple_of(b * 128, 128), 128)
            factor = [kbuf[d, :, at] for d in range(2 * groups)]
            for row in range(0, piece, 16):
                rows = slice(row, row + 16)
                data = [
                    [z_in[0, c, f, k, rows, at].astype(jnp.float32) for k in range(2)]
                    for f in range(groups)
                ]
                for f in range(groups):
                    real, imag = data[f][0] * factor[0], data[f][1] * factor[0]
                    for g in range(groups):
                        if g == f:
                            continue
                        kr, ki = factor[2 * abs(g - f)], factor[2 * abs(g - f) + 1]
                        if g > f:
                            real += kr * data[g][0] - ki * data[g][1]
                            imag += kr * data[g][1] + ki * data[g][0]
                        else:
                            real += kr * data[g][0] + ki * data[g][1]
                            imag += kr * data[g][1] - ki * data[g][0]
                    z_out[1, c, f, 0, rows, at] = real.astype(jnp.bfloat16)
                    z_out[1, c, f, 1, rows, at] = imag.astype(jnp.bfloat16)
            return carry

        lax.fori_loop(0, span // 128, step, 0)

    def shot_operand(c):
        return lambda k, which: xt[c, k, which]

    def data_operand(c):
        for i in range(tiles):
            cols = slice(i * B, (i + 1) * B)
            part = [z_in[1, c, :, k, :, cols].reshape(width, B) for k in range(2)]
            xt[c, i, 0, :width] = part[0]
            xt[c, i, 0, width:] = part[1]
            xt[c, i, 1, :width] = part[1]
            xt[c, i, 1, width:] = -part[0]
        return shot_operand(c)

    def finish(c):
        columns = slice(c * width, (c + 1) * width)
        for j in range(tiles):
            whole, turned = gathered(1, c, j)
            rows = slice(j * B, (j + 1) * B)
            result = (dot_nt(v[0, rows, :], whole) + dot_nt(v[1, rows, :], turned)).astype(
                jnp.bfloat16
            )
            out_ref[0, rows, columns] = result[:, :width]
            out_ref[1, rows, columns] = result[:, width:]

    pl.semaphore_wait(barrier, n + groups - 2)
    produce(0, 0, shot_operand(0), v, True)
    for c in range(1, chunks):
        produce(0, c, shot_operand(c), v, False)

    def follow(phase, c):
        def do(r):
            t_copy(phase, c - 1, r).wait_send()
            t_copy(phase, c, r).start()

        each_send(do)

    loads[2].wait()
    for c in range(chunks):
        if c + 1 < chunks:
            follow(0, c + 1)
        await_tiles(0, c)
        record(c)
        z_start(0, c)
        if c > 0:
            z_wait(1, c - 1)
            produce(1, c - 1, data_operand(c - 1), u, True)
        z_wait(0, c)
        window(c)
        z_start(1, c)
    z_wait(1, chunks - 1)
    produce(1, chunks - 1, data_operand(chunks - 1), u, True)
    for c in range(chunks):
        await_tiles(1, c)
        finish(c)

    each_send(lambda r: t_copy(0, chunks - 1, r).wait_send())
    for c in range(chunks):
        each_send(functools.partial(lambda c, r: t_copy(1, c, r).wait_send(), c))
        for phase in range(2):
            for r in range(1, groups):
                z_copy(phase, c, r).wait_send()


def on_device(sources, u_factor, v_factor, tile_ranks, window_start, window_end):
    n = lax.axis_size("tile")
    groups = lax.axis_size("freq")
    span, shots = sources.shape[2:]
    depth = u_factor.shape[3]
    tiles = span // B
    width = shots // CHUNKS
    piece = width // groups
    lanes = tiles * R
    flops = 4 * 8 * span * depth * shots
    bf16 = jnp.bfloat16
    dma = pltpu.SemaphoreType.DMA
    anywhere = pl.BlockSpec(memory_space=pl.ANY)
    vmem = pl.BlockSpec(memory_space=pltpu.VMEM)
    out = pl.pallas_call(
        functools.partial(kernel, n, groups),
        out_shape=jax.ShapeDtypeStruct((2, span, shots), bf16),
        in_specs=[
            anywhere, anywhere, anywhere, pl.BlockSpec(memory_space=pltpu.SMEM), vmem, vmem,
        ],
        out_specs=vmem,
        scratch_shapes=[
            pltpu.VMEM((2, span, shots), bf16),
            pltpu.VMEM((2, span, depth), bf16),
            pltpu.VMEM((2, span, depth), bf16),
            pltpu.VMEM((CHUNKS, tiles, 2, 2 * width, B), bf16),
            pltpu.VMEM((2, CHUNKS, n, tiles, 2 * width, lanes), bf16),
            pltpu.VMEM((2, CHUNKS, n, tiles, 2 * width, lanes), bf16),
            pltpu.VMEM((2, CHUNKS, groups, 2, piece, span), bf16),
            pltpu.VMEM((2, CHUNKS, groups, 2, piece, span), bf16),
            pltpu.VMEM((2 * groups, 1, span), jnp.float32),
            dma((3,)),
            dma((2, CHUNKS, n)),
            dma((2, CHUNKS, n)),
            dma((2, CHUNKS, groups)),
            dma((2, CHUNKS, groups)),
        ],
        compiler_params=pltpu.CompilerParams(
            collective_id=0, has_side_effects=True, vmem_limit_bytes=56 * 2**20
        ),
        cost_estimate=pl.CostEstimate(
            flops=flops, bytes_accessed=4 * span * (2 * depth + 2 * shots), transcendentals=0
        ),
    )(
        sources[0], u_factor[0], v_factor[0], tile_ranks,
        window_start.reshape(1, span), window_end.reshape(1, span),
    )
    return out[None]


def solution(mesh):
    wide = P("freq", None, "tile", None)
    return jax.shard_map(
        on_device, mesh=mesh, in_specs=(wide, wide, wide, P(), P("tile"), P("tile")),
        out_specs=wide, check_vma=False,
    )
```

```python
import functools
import math

import jax
import jax.numpy as jnp
from jax import lax
from jax.experimental import pallas as pl
from jax.experimental.pallas import tpu as pltpu
from jax.sharding import PartitionSpec as P

B = 256
R = 64
LEAD = 4
MESH = pl.DeviceIdType.MESH


def dot(a, b):
    return jnp.dot(a, b, preferred_element_type=jnp.float32)


def dot_nt(a, b):
    return lax.dot_general(a, b, (((1,), (1,)), ((), ())), preferred_element_type=jnp.float32)


def kernel(
    n, groups, src_hbm, u_hbm, v_hbm, ranks, start_ref, end_ref, out_ref,
    src, u, v, xt, t_out, t_in, z_out, z_in, kbuf,
    in_sem, t_send, t_recv, z_send, z_recv,
):
    me = lax.axis_index("tile")
    mf = lax.axis_index("freq")
    span = src.shape[1]
    shots = src.shape[2]
    tiles = span // B
    lanes = tiles * R
    chunks = t_out.shape[1]
    width = shots // chunks
    piece = width // groups
    pairs = n // 2
    my_pair = lax.div(me, 2)
    sibling = me + 1 - 2 * lax.rem(me, 2)

    barrier = pltpu.get_barrier_semaphore()
    for r in range(1, n):
        pl.semaphore_signal(barrier, inc=1, device_id=(mf, lax.rem(me + r, n)), device_id_type=MESH)
    for r in range(1, groups):
        pl.semaphore_signal(
            barrier, inc=1, device_id=(lax.rem(mf + r, groups), me), device_id_type=MESH
        )
    loads = [
        pltpu.make_async_copy(a, b, in_sem.at[k])
        for k, (a, b) in enumerate(((src_hbm, src), (v_hbm, v), (u_hbm, u)))
    ]
    for copy in loads:
        copy.start()

    times = 2 * groups
    first, last = start_ref[...], end_ref[...]
    inside = [((first <= t) & (last > t)).astype(jnp.float32) for t in range(times)]
    for d in range(groups):
        real = imag = jnp.zeros_like(inside[0])
        for t in range(times):
            angle = 2.0 * math.pi * ((t * d) % times) / times
            real += inside[t] * (math.cos(angle) / groups)
            imag += inside[t] * (math.sin(angle) / groups)
        kbuf[2 * d] = real
        kbuf[2 * d + 1] = imag

    loads[0].wait()
    for c in range(chunks):
        for j in range(tiles):
            part = [
                src[k, j * B : (j + 1) * B, c * width : (c + 1) * width].astype(jnp.float32).T
                for k in range(2)
            ]
            xt[c, j, 0, :width] = part[0].astype(jnp.bfloat16)
            xt[c, j, 0, width:] = part[1].astype(jnp.bfloat16)
            xt[c, j, 1, :width] = part[1].astype(jnp.bfloat16)
            xt[c, j, 1, width:] = (-part[0]).astype(jnp.bfloat16)
    loads[1].wait()

    lane = lax.broadcasted_iota(jnp.int32, (1, lanes), 1)
    low = lane < R
    within = lax.rem(lane, R)

    def t_copy(phase, c, r):
        pair = lax.rem(my_pair + lax.div(r, 2), pairs)
        target = jnp.where(lax.div(r, 2) == 0, sibling, 2 * pair + lax.rem(r, 2))
        return pltpu.make_async_remote_copy(
            src_ref=t_out.at[phase, c, target],
            dst_ref=t_in.at[phase, c, me],
            send_sem=t_send.at[phase, c, r],
            recv_sem=t_recv.at[phase, c, me],
            device_id=(mf, target),
            device_id_type=MESH,
        )

    def t_arrived(phase, c, source):
        return pltpu.make_async_remote_copy(
            src_ref=t_out.at[phase, c, source],
            dst_ref=t_in.at[phase, c, source],
            send_sem=t_send.at[phase, c, 0],
            recv_sem=t_recv.at[phase, c, source],
            device_id=(mf, source),
            device_id_type=MESH,
        )

    def blocks(phase, c, pair, operands, weights, put):
        columns = pl.ds(pl.multiple_of(pair * 2 * lanes, 2 * lanes), 2 * lanes)
        full = [
            dot(operands(k, 0), weights[0, k * B : (k + 1) * B, columns])
            + dot(operands(k, 1), weights[1, k * B : (k + 1) * B, columns])
            for k in range(tiles)
        ]
        for h in range(2):
            dest = 2 * pair + h
            own, other = (f[:, h * lanes : (h + 1) * lanes] for f in full)
            mixed = (
                jnp.where(low, own, pltpu.roll(other, R, 1)),
                jnp.where(low, pltpu.roll(own, R, 1), other),
            )
            for k in range(tiles):
                theirs = dest * tiles + k
                if phase == 0:
                    rank = [ranks[theirs, me * tiles + m] for m in range(tiles)]
                else:
                    rank = [ranks[me * tiles + m, theirs] for m in range(tiles)]
                keep = within < jnp.where(low, rank[0], rank[1])
                put(dest, k, jnp.where(keep, mixed[k], 0.0).astype(jnp.bfloat16))

    def produce(phase, c, operands, weights, send):
        def put(dest, k, value):
            t_out[phase, c, dest, k] = value

        def step(k, carry):
            blocks(phase, c, lax.rem(my_pair + k, pairs), operands, weights, put)
            for h in range(2):
                if send:
                    t_copy(phase, c, 2 * k + h).start()
            return carry

        lax.fori_loop(1, pairs, step, 0)
        blocks(phase, c, my_pair, operands, weights, put)
        t_in[phase, c, me] = t_out[phase, c, me]
        if send:
            t_copy(phase, c, 0).start()

    def each_send(do):
        def step(r, carry):
            do(r)
            return carry

        lax.fori_loop(2, n, step, 0)
        do(0)

    def await_tiles(phase, c):
        def step(r, carry):
            t_arrived(phase, c, lax.rem(me + r, n)).wait_recv()
            return carry

        lax.fori_loop(1, n, step, 0)

    def gathered(phase, c, k):
        whole = jnp.concatenate([t_in[phase, c, s, k] for s in range(n)], axis=1)
        turned = jnp.concatenate([-whole[width:], whole[:width]], axis=0)
        return whole, turned

    def z_copy(phase, c, r):
        target = lax.rem(mf + r, groups)
        return pltpu.make_async_remote_copy(
            src_ref=z_out.at[phase, c, target],
            dst_ref=z_in.at[phase, c, mf],
            send_sem=z_send.at[phase, c, r],
            recv_sem=z_recv.at[phase, c, mf],
            device_id=(target, me),
            device_id_type=MESH,
        )

    def z_arrived(phase, c, source):
        return pltpu.make_async_remote_copy(
            src_ref=z_out.at[phase, c, source],
            dst_ref=z_in.at[phase, c, source],
            send_sem=z_send.at[phase, c, 0],
            recv_sem=z_recv.at[phase, c, source],
            device_id=(source, me),
            device_id_type=MESH,
        )

    def z_start(phase, c):
        for r in range(1, groups):
            z_copy(phase, c, r).start()
        z_in[phase, c, mf] = z_out[phase, c, mf]

    def z_wait(phase, c):
        for r in range(1, groups):
            z_arrived(phase, c, lax.rem(mf + r, groups)).wait_recv()

    def record(c):
        for i in range(tiles):
            whole, turned = gathered(0, c, i)
            rows = slice(i * B, (i + 1) * B)
            result = (dot_nt(whole, u[0, rows, :]) + dot_nt(turned, u[1, rows, :])).astype(
                jnp.bfloat16
            )
            for g in range(groups):
                for k in range(2):
                    at = k * width + g * piece
                    z_out[0, c, g, k, :, rows] = result[at : at + piece]

    def window(c):
        def step(b, carry):
            at = pl.ds(pl.multiple_of(b * 128, 128), 128)
            factor = [kbuf[d, :, at] for d in range(2 * groups)]
            for row in range(0, piece, 16):
                rows = slice(row, row + 16)
                data = [
                    [z_in[0, c, f, k, rows, at].astype(jnp.float32) for k in range(2)]
                    for f in range(groups)
                ]
                for f in range(groups):
                    real, imag = data[f][0] * factor[0], data[f][1] * factor[0]
                    for g in range(groups):
                        if g == f:
                            continue
                        kr, ki = factor[2 * abs(g - f)], factor[2 * abs(g - f) + 1]
                        if g > f:
                            real += kr * data[g][0] - ki * data[g][1]
                            imag += kr * data[g][1] + ki * data[g][0]
                        else:
                            real += kr * data[g][0] + ki * data[g][1]
                            imag += kr * data[g][1] - ki * data[g][0]
                    z_out[1, c, f, 0, rows, at] = real.astype(jnp.bfloat16)
                    z_out[1, c, f, 1, rows, at] = imag.astype(jnp.bfloat16)
            return carry

        lax.fori_loop(0, span // 128, step, 0)

    def shot_operand(c):
        return lambda k, which: xt[c, k, which]

    def data_operand(c):
        for i in range(tiles):
            cols = slice(i * B, (i + 1) * B)
            part = [z_in[1, c, :, k, :, cols].reshape(width, B) for k in range(2)]
            xt[c, i, 0, :width] = part[0]
            xt[c, i, 0, width:] = part[1]
            xt[c, i, 1, :width] = part[1]
            xt[c, i, 1, width:] = -part[0]
        return shot_operand(c)

    def finish(c):
        columns = slice(c * width, (c + 1) * width)
        for j in range(tiles):
            whole, turned = gathered(1, c, j)
            rows = slice(j * B, (j + 1) * B)
            result = (dot_nt(v[0, rows, :], whole) + dot_nt(v[1, rows, :], turned)).astype(
                jnp.bfloat16
            )
            out_ref[0, rows, columns] = result[:, :width]
            out_ref[1, rows, columns] = result[:, width:]

    def begin(c):
        each_send(lambda r: t_copy(0, c, r).start())

    produce(0, 0, shot_operand(0), v, False)
    pl.semaphore_wait(barrier, n + groups - 2)
    begin(0)
    for c in range(1, chunks):
        produce(0, c, shot_operand(c), v, c < LEAD)
    loads[2].wait()
    for step in range(chunks + 4):
        if step < chunks:
            await_tiles(0, step)
            if step + LEAD < chunks:
                begin(step + LEAD)
            record(step)
            z_start(0, step)
        if 0 <= step - 1 < chunks:
            z_wait(0, step - 1)
            window(step - 1)
            z_start(1, step - 1)
        if 0 <= step - 2 < chunks:
            z_wait(1, step - 2)
            produce(1, step - 2, data_operand(step - 2), u, True)
        if 0 <= step - 4 < chunks:
            await_tiles(1, step - 4)
            finish(step - 4)

    for c in range(chunks):
        for phase in range(2):
            each_send(lambda r, phase=phase, c=c: t_copy(phase, c, r).wait_send())
            for r in range(1, groups):
                z_copy(phase, c, r).wait_send()


def on_device(sources, u_factor, v_factor, tile_ranks, window_start, window_end):
    n = lax.axis_size("tile")
    groups = lax.axis_size("freq")
    span, shots = sources.shape[2:]
    depth = u_factor.shape[3]
    tiles = span // B
    chunks = max(1, shots // (16 * groups))
    width = shots // chunks
    piece = width // groups
    lanes = tiles * R
    flops = 4 * 8 * span * depth * shots
    bf16 = jnp.bfloat16
    dma = pltpu.SemaphoreType.DMA
    anywhere = pl.BlockSpec(memory_space=pl.ANY)
    vmem = pl.BlockSpec(memory_space=pltpu.VMEM)
    out = pl.pallas_call(
        functools.partial(kernel, n, groups),
        out_shape=jax.ShapeDtypeStruct((2, span, shots), bf16),
        in_specs=[
            anywhere, anywhere, anywhere, pl.BlockSpec(memory_space=pltpu.SMEM), vmem, vmem,
        ],
        out_specs=vmem,
        scratch_shapes=[
            pltpu.VMEM((2, span, shots), bf16),
            pltpu.VMEM((2, span, depth), bf16),
            pltpu.VMEM((2, span, depth), bf16),
            pltpu.VMEM((chunks, tiles, 2, 2 * width, B), bf16),
            pltpu.VMEM((2, chunks, n, tiles, 2 * width, lanes), bf16),
            pltpu.VMEM((2, chunks, n, tiles, 2 * width, lanes), bf16),
            pltpu.VMEM((2, chunks, groups, 2, piece, span), bf16),
            pltpu.VMEM((2, chunks, groups, 2, piece, span), bf16),
            pltpu.VMEM((2 * groups, 1, span), jnp.float32),
            dma((3,)),
            dma((2, chunks, n)),
            dma((2, chunks, n)),
            dma((2, chunks, groups)),
            dma((2, chunks, groups)),
        ],
        compiler_params=pltpu.CompilerParams(
            collective_id=0, has_side_effects=True, vmem_limit_bytes=56 * 2**20
        ),
        cost_estimate=pl.CostEstimate(
            flops=flops, bytes_accessed=4 * span * (2 * depth + 2 * shots), transcendentals=0
        ),
    )(
        sources[0], u_factor[0], v_factor[0], tile_ranks,
        window_start.reshape(1, span), window_end.reshape(1, span),
    )
    return out[None]


def solution(mesh):
    wide = P("freq", None, "tile", None)
    return jax.shard_map(
        on_device, mesh=mesh, in_specs=(wide, wide, wide, P(), P("tile"), P("tile")),
        out_specs=wide, check_vma=False,
    )
```

```python
import functools
import math

import jax
import jax.numpy as jnp
from jax import lax
from jax.experimental import pallas as pl
from jax.experimental.pallas import tpu as pltpu
from jax.sharding import PartitionSpec as P

B = 256
R = 64
LEAD = 4
MESH = pl.DeviceIdType.MESH


def dot(a, b):
    return jnp.dot(a, b, preferred_element_type=jnp.float32)


def dot_nt(a, b):
    return lax.dot_general(a, b, (((1,), (1,)), ((), ())), preferred_element_type=jnp.float32)


def kernel(
    n, groups, src_hbm, u_hbm, v_hbm, ranks, start_ref, end_ref, out_ref,
    src, u, v, xt, t_out, t_in, z_out, z_in, kbuf,
    in_sem, t_send, t_recv, z_send, z_recv,
):
    me = lax.axis_index("tile")
    mf = lax.axis_index("freq")
    span = src.shape[1]
    shots = src.shape[2]
    tiles = span // B
    lanes = tiles * R
    chunks = t_out.shape[1]
    width = shots // chunks
    piece = width // groups
    pairs = n // 2
    my_pair = lax.div(me, 2)
    sibling = me + 1 - 2 * lax.rem(me, 2)

    barrier = pltpu.get_barrier_semaphore()
    for r in range(1, n):
        pl.semaphore_signal(barrier, inc=1, device_id=(mf, lax.rem(me + r, n)), device_id_type=MESH)
    for r in range(1, groups):
        pl.semaphore_signal(
            barrier, inc=1, device_id=(lax.rem(mf + r, groups), me), device_id_type=MESH
        )
    loads = [
        pltpu.make_async_copy(a, b, in_sem.at[k])
        for k, (a, b) in enumerate(((src_hbm, src), (v_hbm, v), (u_hbm, u)))
    ]
    for copy in loads:
        copy.start()

    loads[0].wait()
    def turn(c):
        for j in range(tiles):
            part = [
                src[k, j * B : (j + 1) * B, c * width : (c + 1) * width].astype(jnp.float32).T
                for k in range(2)
            ]
            xt[c, j, 0, :width] = part[0].astype(jnp.bfloat16)
            xt[c, j, 0, width:] = part[1].astype(jnp.bfloat16)
            xt[c, j, 1, :width] = part[1].astype(jnp.bfloat16)
            xt[c, j, 1, width:] = (-part[0]).astype(jnp.bfloat16)

    turn(0)
    loads[1].wait()

    lane = lax.broadcasted_iota(jnp.int32, (1, lanes), 1)
    low = lane < R
    within = lax.rem(lane, R)

    def t_copy(phase, c, r):
        pair = lax.rem(my_pair + lax.div(r, 2), pairs)
        target = jnp.where(lax.div(r, 2) == 0, sibling, 2 * pair + lax.rem(r, 2))
        return pltpu.make_async_remote_copy(
            src_ref=t_out.at[phase, c, target],
            dst_ref=t_in.at[phase, c, me],
            send_sem=t_send.at[phase, c, r],
            recv_sem=t_recv.at[phase, c, me],
            device_id=(mf, target),
            device_id_type=MESH,
        )

    def t_arrived(phase, c, source):
        return pltpu.make_async_remote_copy(
            src_ref=t_out.at[phase, c, source],
            dst_ref=t_in.at[phase, c, source],
            send_sem=t_send.at[phase, c, 0],
            recv_sem=t_recv.at[phase, c, source],
            device_id=(mf, source),
            device_id_type=MESH,
        )

    def blocks(phase, c, pair, operands, weights, put):
        columns = pl.ds(pl.multiple_of(pair * 2 * lanes, 2 * lanes), 2 * lanes)
        full = [
            dot(operands(k, 0), weights[0, k * B : (k + 1) * B, columns])
            + dot(operands(k, 1), weights[1, k * B : (k + 1) * B, columns])
            for k in range(tiles)
        ]
        for h in range(2):
            dest = 2 * pair + h
            own, other = (f[:, h * lanes : (h + 1) * lanes] for f in full)
            mixed = (
                jnp.where(low, own, pltpu.roll(other, R, 1)),
                jnp.where(low, pltpu.roll(own, R, 1), other),
            )
            for k in range(tiles):
                theirs = dest * tiles + k
                if phase == 0:
                    rank = [ranks[theirs, me * tiles + m] for m in range(tiles)]
                else:
                    rank = [ranks[me * tiles + m, theirs] for m in range(tiles)]
                keep = within < jnp.where(low, rank[0], rank[1])
                put(dest, k, jnp.where(keep, mixed[k], 0.0).astype(jnp.bfloat16))

    def produce(phase, c, operands, weights, send):
        def put(dest, k, value):
            t_out[phase, c, dest, k] = value

        def step(k, carry):
            blocks(phase, c, lax.rem(my_pair + k, pairs), operands, weights, put)
            for h in range(2):
                if send:
                    t_copy(phase, c, 2 * k + h).start()
            return carry

        lax.fori_loop(1, pairs, step, 0)
        blocks(phase, c, my_pair, operands, weights, put)
        t_in[phase, c, me] = t_out[phase, c, me]
        if send:
            t_copy(phase, c, 0).start()

    def each_send(do):
        def step(r, carry):
            do(r)
            return carry

        lax.fori_loop(2, n, step, 0)
        do(0)

    def await_tiles(phase, c):
        def step(r, carry):
            t_arrived(phase, c, lax.rem(me + r, n)).wait_recv()
            return carry

        lax.fori_loop(1, n, step, 0)

    def gathered(phase, c, k):
        whole = jnp.concatenate([t_in[phase, c, s, k] for s in range(n)], axis=1)
        turned = jnp.concatenate([-whole[width:], whole[:width]], axis=0)
        return whole, turned

    def z_copy(phase, c, r):
        target = lax.rem(mf + r, groups)
        return pltpu.make_async_remote_copy(
            src_ref=z_out.at[phase, c, target],
            dst_ref=z_in.at[phase, c, mf],
            send_sem=z_send.at[phase, c, r],
            recv_sem=z_recv.at[phase, c, mf],
            device_id=(target, me),
            device_id_type=MESH,
        )

    def z_arrived(phase, c, source):
        return pltpu.make_async_remote_copy(
            src_ref=z_out.at[phase, c, source],
            dst_ref=z_in.at[phase, c, source],
            send_sem=z_send.at[phase, c, 0],
            recv_sem=z_recv.at[phase, c, source],
            device_id=(source, me),
            device_id_type=MESH,
        )

    def z_start(phase, c):
        for r in range(1, groups):
            z_copy(phase, c, r).start()
        z_in[phase, c, mf] = z_out[phase, c, mf]

    def z_wait(phase, c):
        for r in range(1, groups):
            z_arrived(phase, c, lax.rem(mf + r, groups)).wait_recv()

    def record(c):
        for i in range(tiles):
            whole, turned = gathered(0, c, i)
            rows = slice(i * B, (i + 1) * B)
            result = (dot_nt(whole, u[0, rows, :]) + dot_nt(turned, u[1, rows, :])).astype(
                jnp.bfloat16
            )
            for g in range(groups):
                for k in range(2):
                    at = k * width + g * piece
                    z_out[0, c, g, k, :, rows] = result[at : at + piece]

    def window(c):
        def step(b, carry):
            at = pl.ds(pl.multiple_of(b * 128, 128), 128)
            factor = [kbuf[d, :, at] for d in range(2 * groups)]
            for row in range(0, piece, 16):
                rows = slice(row, row + 16)
                data = [
                    [z_in[0, c, f, k, rows, at].astype(jnp.float32) for k in range(2)]
                    for f in range(groups)
                ]
                for f in range(groups):
                    real, imag = data[f][0] * factor[0], data[f][1] * factor[0]
                    for g in range(groups):
                        if g == f:
                            continue
                        kr, ki = factor[2 * abs(g - f)], factor[2 * abs(g - f) + 1]
                        if g > f:
                            real += kr * data[g][0] - ki * data[g][1]
                            imag += kr * data[g][1] + ki * data[g][0]
                        else:
                            real += kr * data[g][0] + ki * data[g][1]
                            imag += kr * data[g][1] - ki * data[g][0]
                    z_out[1, c, f, 0, rows, at] = real.astype(jnp.bfloat16)
                    z_out[1, c, f, 1, rows, at] = imag.astype(jnp.bfloat16)
            return carry

        lax.fori_loop(0, span // 128, step, 0)

    def shot_operand(c):
        return lambda k, which: xt[c, k, which]

    def data_operand(c):
        for i in range(tiles):
            cols = slice(i * B, (i + 1) * B)
            part = [z_in[1, c, :, k, :, cols].reshape(width, B) for k in range(2)]
            xt[c, i, 0, :width] = part[0]
            xt[c, i, 0, width:] = part[1]
            xt[c, i, 1, :width] = part[1]
            xt[c, i, 1, width:] = -part[0]
        return shot_operand(c)

    def finish(c):
        columns = slice(c * width, (c + 1) * width)
        for j in range(tiles):
            whole, turned = gathered(1, c, j)
            rows = slice(j * B, (j + 1) * B)
            result = (dot_nt(v[0, rows, :], whole) + dot_nt(v[1, rows, :], turned)).astype(
                jnp.bfloat16
            )
            out_ref[0, rows, columns] = result[:, :width]
            out_ref[1, rows, columns] = result[:, width:]

    def begin(c):
        each_send(lambda r: t_copy(0, c, r).start())

    produce(0, 0, shot_operand(0), v, False)
    pl.semaphore_wait(barrier, n + groups - 2)
    begin(0)
    for c in range(1, chunks):
        turn(c)
        produce(0, c, shot_operand(c), v, c < LEAD)
    times = 2 * groups
    first, last = start_ref[...], end_ref[...]
    inside = [((first <= t) & (last > t)).astype(jnp.float32) for t in range(times)]
    for d in range(groups):
        real = imag = jnp.zeros_like(inside[0])
        for t in range(times):
            angle = 2.0 * math.pi * ((t * d) % times) / times
            real += inside[t] * (math.cos(angle) / groups)
            imag += inside[t] * (math.sin(angle) / groups)
        kbuf[2 * d] = real
        kbuf[2 * d + 1] = imag

    loads[2].wait()
    for step in range(chunks + 4):
        if step < chunks:
            await_tiles(0, step)
            if step + LEAD < chunks:
                begin(step + LEAD)
            record(step)
            z_start(0, step)
        if 0 <= step - 1 < chunks:
            z_wait(0, step - 1)
            window(step - 1)
            z_start(1, step - 1)
        if 0 <= step - 2 < chunks:
            z_wait(1, step - 2)
            produce(1, step - 2, data_operand(step - 2), u, True)
        if 0 <= step - 4 < chunks:
            await_tiles(1, step - 4)
            finish(step - 4)

    for c in range(chunks):
        for phase in range(2):
            each_send(lambda r, phase=phase, c=c: t_copy(phase, c, r).wait_send())
            for r in range(1, groups):
                z_copy(phase, c, r).wait_send()


def on_device(sources, u_factor, v_factor, tile_ranks, window_start, window_end):
    n = lax.axis_size("tile")
    groups = lax.axis_size("freq")
    span, shots = sources.shape[2:]
    depth = u_factor.shape[3]
    tiles = span // B
    chunks = max(1, shots // (16 * groups))
    width = shots // chunks
    piece = width // groups
    lanes = tiles * R
    flops = 4 * 8 * span * depth * shots
    bf16 = jnp.bfloat16
    dma = pltpu.SemaphoreType.DMA
    anywhere = pl.BlockSpec(memory_space=pl.ANY)
    vmem = pl.BlockSpec(memory_space=pltpu.VMEM)
    out = pl.pallas_call(
        functools.partial(kernel, n, groups),
        out_shape=pltpu.VMEM((2, span, shots), bf16),
        in_specs=[
            anywhere, anywhere, anywhere, pl.BlockSpec(memory_space=pltpu.SMEM), vmem, vmem,
        ],
        out_specs=vmem,
        scratch_shapes=[
            pltpu.VMEM((2, span, shots), bf16),
            pltpu.VMEM((2, span, depth), bf16),
            pltpu.VMEM((2, span, depth), bf16),
            pltpu.VMEM((chunks, tiles, 2, 2 * width, B), bf16),
            pltpu.VMEM((2, chunks, n, tiles, 2 * width, lanes), bf16),
            pltpu.VMEM((2, chunks, n, tiles, 2 * width, lanes), bf16),
            pltpu.VMEM((2, chunks, groups, 2, piece, span), bf16),
            pltpu.VMEM((2, chunks, groups, 2, piece, span), bf16),
            pltpu.VMEM((2 * groups, 1, span), jnp.float32),
            dma((3,)),
            dma((2, chunks, n)),
            dma((2, chunks, n)),
            dma((2, chunks, groups)),
            dma((2, chunks, groups)),
        ],
        compiler_params=pltpu.CompilerParams(
            collective_id=0, has_side_effects=True, vmem_limit_bytes=60 * 2**20
        ),
        cost_estimate=pl.CostEstimate(
            flops=flops, bytes_accessed=4 * span * (2 * depth + 2 * shots), transcendentals=0
        ),
    )(
        sources[0], u_factor[0], v_factor[0], tile_ranks,
        window_start.reshape(1, span), window_end.reshape(1, span),
    )
    return out[None]


def solution(mesh):
    wide = P("freq", None, "tile", None)
    return jax.shard_map(
        on_device, mesh=mesh, in_specs=(wide, wide, wide, P(), P("tile"), P("tile")),
        out_specs=wide, check_vma=False,
    )
```
